256 devices in a mesh: doc: 16 (over z_hi, x, core), seq: 16 (over z_lo, y).
Axes of the slice: x: 4, y: 4, z: 8 (z_hi: 2, z_lo: 4; z = z_hi * 4 + z_lo), core: 2. Of those that a mesh axis runs over, the one named last changes fastest.
Arguments:
- queries: bfloat16 [16, 2048, 2048], P('doc', 'seq'), may hold values from -6 to 6
- keys: bfloat16 [16, 2048, 512], P('doc', 'seq'), may hold values from -6 to 6
- values: bfloat16 [16, 2048, 512], P('doc', 'seq'), may hold values from -6 to 6
- outputs: bfloat16 [16, 2048, 2048], P('doc', 'seq'), may hold values from -1.5 to 1.5
- out_grads: bfloat16 [16, 2048, 2048], P('doc', 'seq'), may hold values from -6 to 6
- lengths: int32 [16, 16, 16], P('doc', 'seq'), may hold values from 1 to 16, 128 in all within a row
- owners: int32 [16, 16, 16], P('doc', 'seq'), may hold values from 0 to 15, each once within a row
Outputs:
- returned: bfloat16 [16, 16, 16, 16, 3072], P('doc', 'seq')
The draws below stay inside these ranges and needn't reach their ends.
Inputs may be any that keep to these rules, and one draw needn't show every extreme that they name: Within each block of 128 positions the 16 lengths sum to 128, and the longest is exactly 16. Within each block the 16 child summaries have 16 different owners.
All inputs are finite; a program needn't handle non-finite values.
Results may differ from the reference program's by a relative error of at most 0.0095.
Values may be sent and summed in bfloat16 or wider, within the bound.
No kernel may reach another device: no remote copies, remote signals or barrier semaphores. Data moves between devices by JAX's collectives and lax.ppermute only.
A program may use at most 64 MiB of HBM per device.

```python
import math
import jax
import jax.numpy as jnp
import numpy as np
from jax import lax

HD = 128
QH = 16
KVH = 4
TOK_DEV = 128
SEQ_LEN = 2048
CAP = 16
N_DOC = 16
N_SEQ = 16


def draw_queries(key, part):
    key = jax.random.fold_in(key, 11)
    shape = (N_DOC, SEQ_LEN, QH, HD)
    drawn = jnp.clip(jax.random.normal(key, shape, jnp.float32), -6.0, 6.0)
    return drawn.reshape(N_DOC, SEQ_LEN, QH * HD).astype(jnp.bfloat16)


def draw_keys(key, part):
    key = jax.random.fold_in(key, 23)
    shape = (N_DOC, SEQ_LEN, KVH, HD)
    drawn = jnp.clip(jax.random.normal(key, shape, jnp.float32), -6.0, 6.0)
    return drawn.reshape(N_DOC, SEQ_LEN, KVH * HD).astype(jnp.bfloat16)


def block_levels(rng, dims, shards, least, high):
    gain, own = 1.0, jax.random.fold_in(rng, 6)
    for axis_at, shards_of in shards:
        steps = jnp.exp(jax.random.uniform(jax.random.fold_in(own, axis_at), (shards_of,), jnp.float32, least / len(shards), high / len(shards)))
        gain = gain * jnp.repeat(steps, dims[axis_at] // shards_of).reshape([-1 if axis == axis_at else 1 for axis in range(len(dims))])
    return gain


def length_profile(number_of, total, limit, slope):
    loads = [(1 << 20) // math.isqrt(rank ** slope) + 1 for rank in range(2, number_of + 1)]
    spare, given = total - limit - (number_of - 1), [1] * (number_of - 1)
    while spare > 0:
        free = [i for i in range(number_of - 1) if given[i] < limit]
        mass, budget = sum([loads[i] for i in free]), spare
        for i in free:
            extra = min(limit - given[i], max(1, budget * loads[i] // mass), spare)
            given[i] = given[i] + extra
            spare = spare - extra
    return np.array([limit] + given)


def ragged(rng, number_of, total, limit, lean):
    if number_of == 2:
        one = jax.random.randint(rng, (), max(1, total - limit), min(limit, total - 1) + 1)
        return jnp.stack([one, total - one])
    sizes = jnp.asarray(length_profile(number_of, total, limit, lean), jnp.int32)
    couples = (number_of - 1) // 2
    giver, sink = sizes[1:1 + 2 * couples:2], sizes[2:2 + 2 * couples:2]
    margin = jnp.minimum(giver - 1, limit - sink)
    moved = jax.random.randint(jax.random.fold_in(rng, 1), (couples,), 0, 1 << 20) % (margin + 1)
    sizes = sizes.at[1:1 + 2 * couples:2].set(giver - moved).at[2:2 + 2 * couples:2].set(sink + moved)
    return sizes[jax.random.permutation(jax.random.fold_in(rng, 2), number_of)]


def centred(stream_key, shape, deviation, most, cuts=(), kind=jnp.bfloat16):
    factor_of = block_levels(stream_key, shape, cuts, -0.22, 0.18) if cuts else 1.0
    values = jax.random.normal(stream_key, shape, jnp.float32) * deviation * factor_of
    return jnp.minimum(jnp.maximum(values, -most), most).astype(kind)


def setup_inputs(seed: int = 0) -> dict:
    seeds = jax.random.split(jax.random.key(seed), 8)
    return {
        "queries": draw_queries(jax.random.fold_in(seeds[7], 71), 0),
        "keys": draw_keys(jax.random.fold_in(seeds[7], 71), 0),
        "values": centred(seeds[2], (N_DOC, SEQ_LEN, KVH * HD), 1.0, 6.0, ((0, 16), (1, 16))),
        "outputs": centred(seeds[3], (N_DOC, SEQ_LEN, QH * HD), 0.25, 1.5, ((0, 16), (1, 16))),
        "out_grads": centred(seeds[4], (N_DOC, SEQ_LEN, QH * HD), 1.0, 6.0, ((0, 16), (1, 16))),
        "lengths": jax.vmap(lambda own: ragged(own, N_DOC, TOK_DEV, CAP, 1))(jax.random.split(seeds[5], N_DOC * N_SEQ)).reshape((N_DOC, N_SEQ, N_DOC)).astype(jnp.int32),
        "owners": jax.vmap(lambda own: jax.random.permutation(own, N_DOC))(jax.random.split(seeds[6], N_DOC * N_SEQ)).reshape((N_DOC, N_SEQ, N_DOC)).astype(jnp.int32),
    }


def head_grads(query_rows, key_rows, value_rows, grad_out, row_terms):
    length = query_rows.shape[0]
    head_dim = query_rows.shape[1]
    blocks = 1
    while blocks < 8 and length // (blocks * 2) >= 512:
        blocks = blocks * 2
    block_rows = length // blocks
    factor = head_dim ** -0.5
    key_acc = jnp.zeros((length, head_dim), jnp.float32)
    value_acc = jnp.zeros((length, head_dim), jnp.float32)
    pieces = []
    for block_id in range(blocks):
        first = block_id * block_rows
        key_end = first + block_rows
        query_blk = query_rows[first:key_end]
        grad_blk = grad_out[first:key_end]
        key_seen = key_rows[:key_end]
        value_seen = value_rows[:key_end]
        score = lax.dot_general(query_blk, key_seen, (((1,), (1,)), ((), ())), preferred_element_type=jnp.float32) * factor
        causal = jnp.arange(key_end)[None, :] <= (first + jnp.arange(block_rows))[:, None]
        score = jnp.where(causal, score, -jnp.inf)
        row_max = jnp.max(score, axis=1, keepdims=True)
        weight = jnp.exp(score - row_max)
        attn_prob = weight / jnp.sum(weight, axis=1, keepdims=True)
        attn_low = attn_prob.astype(jnp.bfloat16)
        grad_prob = lax.dot_general(grad_blk, value_seen, (((1,), (1,)), ((), ())), preferred_element_type=jnp.float32)
        grad_score = (attn_prob * (grad_prob - row_terms[first:key_end][:, None])).astype(jnp.bfloat16)
        pieces.append((jnp.dot(grad_score, key_seen, preferred_element_type=jnp.float32) * factor).astype(jnp.bfloat16))
        key_part = lax.dot_general(grad_score, query_blk, (((0,), (0,)), ((), ())), preferred_element_type=jnp.float32)
        value_part = lax.dot_general(attn_low, grad_blk, (((0,), (0,)), ((), ())), preferred_element_type=jnp.float32)
        missing = length - key_end
        key_acc = key_acc + jnp.pad(key_part, ((0, missing), (0, 0)))
        value_acc = value_acc + jnp.pad(value_part, ((0, missing), (0, 0)))
    return jnp.concatenate(pieces, axis=0), (key_acc * factor).astype(jnp.bfloat16), value_acc.astype(jnp.bfloat16)


def route(grad_rows, child_lens, child_owner, doc_devs, capacity):
    child_start = jnp.cumsum(child_lens) - child_lens
    owned = child_owner[None, :] == jnp.arange(doc_devs, dtype=jnp.int32)[:, None]
    start_of = jnp.sum(jnp.where(owned, child_start[None, :], 0), axis=1)
    len_of = jnp.sum(jnp.where(owned, child_lens[None, :], 0), axis=1)
    slot_ids = jnp.arange(capacity, dtype=jnp.int32)
    filled = slot_ids[None, :] < len_of[:, None]
    row_ids = jnp.where(filled, start_of[:, None] + slot_ids[None, :], 0).astype(jnp.int32)
    picked = jnp.take(grad_rows, row_ids.reshape(-1), axis=0).reshape(doc_devs, capacity, grad_rows.shape[1])
    return jnp.where(filled[:, :, None], picked, jnp.zeros_like(picked))


def doc_rows(arrays):
    queries_d, keys_d, values_d, outputs_d, grads_d = arrays
    length = queries_d.shape[0]
    group = QH // KVH
    slots = np.arange(QH) // group
    query_heads = queries_d.reshape(length, QH, HD).transpose(1, 0, 2)
    key_heads = keys_d.reshape(length, KVH, HD)[:, slots].transpose(1, 0, 2)
    value_heads = values_d.reshape(length, KVH, HD)[:, slots].transpose(1, 0, 2)
    grad_heads = grads_d.reshape(length, QH, HD).transpose(1, 0, 2)
    row_terms = jnp.sum(grads_d.astype(jnp.float32).reshape(length, QH, HD) * outputs_d.astype(jnp.float32).reshape(length, QH, HD), axis=2).T
    query_grad, key_parts, value_parts = lax.map(lambda items: head_grads(*items), (query_heads, key_heads, value_heads, grad_heads, row_terms))
    key_grad = jnp.sum(key_parts.astype(jnp.float32).reshape(KVH, group, length, HD), axis=1).astype(jnp.bfloat16)
    value_grad = jnp.sum(value_parts.astype(jnp.float32).reshape(KVH, group, length, HD), axis=1).astype(jnp.bfloat16)
    return jnp.concatenate([query_grad.transpose(1, 0, 2).reshape(length, QH * HD), key_grad.transpose(1, 0, 2).reshape(length, KVH * HD), value_grad.transpose(1, 0, 2).reshape(length, KVH * HD)], axis=1)


def reference(queries, keys, values, outputs, out_grads, lengths, owners):
    all_rows = lax.map(doc_rows, (queries, keys, values, outputs, out_grads))
    blocked = all_rows.reshape(N_DOC, N_SEQ, TOK_DEV, all_rows.shape[2])
    routed = jax.vmap(jax.vmap(lambda rows_in, lens_in, owners_in: route(rows_in, lens_in, owners_in, N_DOC, CAP)))(blocked, lengths, owners)
    return routed.transpose(2, 1, 0, 3, 4)
```

```python
import functools

import jax
import jax.numpy as jnp
from jax import lax
from jax.experimental import pallas as pl
from jax.experimental.pallas import tpu as pltpu
from jax.sharding import Mesh, PartitionSpec as P

HD = 128
QH = 16
KVH = 4
GROUP = QH // KVH
TOK = 128
CAP = 16
SLOTS = 4
BLK = SLOTS * TOK
QROWS = GROUP * TOK
QD_ROWS = 2 * QROWS + 16
KV_ROWS = 2 * TOK
FACTOR = HD ** (-0.5)
LOG2E = 1.4426950408889634
f32 = jnp.float32
bf16 = jnp.bfloat16
VMEM = pl.BlockSpec(memory_space=pltpu.VMEM)
SMEM = pl.BlockSpec(memory_space=pltpu.SMEM)
PARAMS = pltpu.CompilerParams(vmem_limit_bytes=56 * 1024 * 1024)


def aligned(index, unit):
    return pl.ds(pl.multiple_of(index * unit, unit), unit)


def split_kv(at_ref, k_ref, v_ref, *outs):
    y = at_ref[0]
    for slot in range(SLOTS):
        head = aligned(lax.rem(y + slot, SLOTS), HD)
        outs[slot][:TOK, :] = k_ref[:, head]
        outs[slot][TOK:, :] = v_ref[:, head]


def split_qd(at_ref, q_ref, o_ref, g_ref, *outs):
    y = at_ref[0]
    lane = lax.broadcasted_iota(jnp.int32, (TOK, HD), 1)
    for slot in range(SLOTS):
        dest = lax.rem(y + slot, SLOTS)
        terms = jnp.zeros((TOK, HD), f32)
        for h in range(GROUP):
            head = aligned(dest * GROUP + h, HD)
            grad = g_ref[:, head]
            outs[slot][h * TOK : (h + 1) * TOK, :] = q_ref[:, head]
            outs[slot][QROWS + h * TOK : QROWS + (h + 1) * TOK, :] = grad
            term = jnp.sum(
                grad.astype(f32) * o_ref[:, head].astype(f32), axis=1, keepdims=True
            )
            terms = jnp.where(lax.rem(lane, GROUP) == h, term, terms)
        high = terms.astype(bf16).astype(f32)
        mid = (terms - high).astype(bf16).astype(f32)
        low = terms - high - mid
        part = lane // GROUP
        packed = jnp.where(
            part == 0, high, jnp.where(part == 1, mid, jnp.where(part == 2, low, 0.0))
        )
        outs[slot][2 * QROWS :, :] = packed.T[:16, :].astype(bf16)


def dot(a, b, dims):
    return lax.dot_general(a, b, (dims, ((), ())), preferred_element_type=f32)


def attention_grads(at_ref, *refs):
    qd_refs, kv_refs = refs[:4], refs[4:8]
    dq_refs, dkv_refs = refs[8:12], refs[12:16]
    qd, kk, vv, score, kacc, vacc, dqs = refs[16:]
    y, z = at_ref[0], at_ref[1]
    for s in range(SLOTS):
        qd[s] = qd_refs[s][...]
    for d in range(SLOTS):
        for s in range(SLOTS):
            kk[d, s * TOK : (s + 1) * TOK, :] = kv_refs[d][s * KV_ROWS : s * KV_ROWS + TOK, :]
            vv[d, s * TOK : (s + 1) * TOK, :] = kv_refs[d][s * KV_ROWS + TOK : (s + 1) * KV_ROWS, :]
    kacc[...] = jnp.zeros_like(kacc)
    vacc[...] = jnp.zeros_like(vacc)

    def tile(slot, carry):
        query = qd[slot, :QROWS, :]
        grad = qd[slot, QROWS : 2 * QROWS, :]
        terms3 = qd[slot, 2 * QROWS :, :].astype(f32)
        term4 = terms3[0:4] + terms3[4:8] + terms3[8:12]
        term = jnp.concatenate([term4[h : h + 1] for h in range(GROUP)], axis=1)
        key_row = lax.broadcasted_iota(jnp.int32, (BLK, QROWS), 0)
        query_col = lax.broadcasted_iota(jnp.int32, (BLK, QROWS), 1)
        key_pos = lax.rem(y + SLOTS - key_row // TOK, SLOTS) * TOK + lax.rem(key_row, TOK)
        query_pos = lax.rem(y + SLOTS - slot, SLOTS) * TOK + lax.rem(query_col, TOK)
        first = dot(kk[0], query, ((1,), (1,)))
        first = jnp.where(key_pos <= query_pos, first, -jnp.inf)
        score[0] = first

        def scores(d, top):
            s = dot(kk[d], query, ((1,), (1,)))
            score[d] = s
            return jnp.maximum(top, jnp.max(s, axis=0, keepdims=True))

        top = lax.fori_loop(1, z + 1, scores, jnp.max(first, axis=0, keepdims=True))

        def weights(d, total):
            e = jnp.exp2((score[d] - top) * (FACTOR * LOG2E))
            score[d] = e
            return total + jnp.sum(e, axis=0, keepdims=True)

        total = lax.fori_loop(0, z + 1, weights, jnp.zeros((1, QROWS), f32))
        inverse = 1.0 / total

        def grads(d, dq):
            attn = score[d] * inverse
            grad_attn = dot(vv[d], grad, ((1,), (1,)))
            low = (attn * (grad_attn - term)).astype(bf16)
            vacc[d] += dot(attn.astype(bf16), grad, ((1,), (0,)))
            kacc[d] += dot(low, query, ((1,), (0,)))
            return dq + dot(low, kk[d], ((0,), (0,)))

        dq = lax.fori_loop(0, z + 1, grads, jnp.zeros((QROWS, HD), f32))
        dqs[slot] = (dq * FACTOR).astype(bf16)
        return carry

    lax.fori_loop(0, SLOTS, tile, 0)
    for s in range(SLOTS):
        dq_refs[s][...] = dqs[s]
    for d in range(SLOTS):
        for s in range(SLOTS):
            rows = slice(s * TOK, (s + 1) * TOK)
            dkv_refs[d][s * KV_ROWS : s * KV_ROWS + TOK, :] = (kacc[d, rows, :] * FACTOR).astype(bf16)
            dkv_refs[d][s * KV_ROWS + TOK : (s + 1) * KV_ROWS, :] = vacc[d, rows, :].astype(bf16)


def pack_query(at_ref, sel_ref, *refs):
    y = at_ref[0]
    parts, outs = refs[:8], refs[8:]
    for doc in range(2):
        sel = sel_ref[doc]
        for slot in range(SLOTS):
            group = lax.rem(y + slot, SLOTS)
            for h in range(GROUP):
                rows = parts[doc * SLOTS + slot][h * TOK : (h + 1) * TOK, :]
                picked = dot(sel, rows, ((1,), (0,))).astype(bf16)
                for dest in range(8):
                    outs[dest][doc, :, aligned(group * GROUP + h, HD)] = picked[
                        dest * CAP : (dest + 1) * CAP
                    ]


def pack_kv(at_ref, sel_ref, *refs):
    y = at_ref[0]
    parts, outs = refs[:2], refs[2:]
    for doc in range(2):
        sel = sel_ref[doc]
        for slot in range(SLOTS):
            head = lax.rem(y + slot, SLOTS)
            for kind in range(2):
                first = slot * KV_ROWS + kind * TOK
                picked = dot(sel, parts[doc][first : first + TOK, :], ((1,), (0,))).astype(bf16)
                for dest in range(8):
                    outs[dest][doc, :, aligned(kind * KVH + head, HD)] = picked[
                        dest * CAP : (dest + 1) * CAP
                    ]


def place(at_ref, *refs):
    queries, kvs, out, sem = refs[:8], refs[8:16], refs[16], refs[17]
    x, c, zh = at_ref[2], at_ref[3], at_ref[4]
    copies = []
    for kx in range(4):
        for cc in range(2):
            piece = kx * 2 + cc
            for dz in range(2):
                doc = lax.rem(zh + dz, 2) * 8 + lax.rem(x + 4 - kx, 4) * 2 + lax.rem(c + cc, 2)
                for source, columns in (
                    (queries[piece], pl.ds(0, QH * HD)),
                    (kvs[piece], pl.ds(QH * HD, 2 * KVH * HD)),
                ):
                    copies.append(
                        pltpu.make_async_copy(
                            source.at[dz], out.at[doc, :, columns], sem.at[len(copies)]
                        )
                    )
    for copy in copies:
        copy.start()
    for copy in copies:
        copy.wait()


def call(kernel, ins, outs, scratch=(), out_specs=None):
    return pl.pallas_call(
        kernel,
        out_shape=outs,
        in_specs=[SMEM] + [VMEM] * ins,
        out_specs=out_specs or [VMEM] * len(outs),
        scratch_shapes=list(scratch),
        compiler_params=PARAMS,
    )


def shaped(*shape, dtype=bf16):
    return jax.ShapeDtypeStruct(shape, dtype)


def selection(lens, owners, targets):
    before = jnp.arange(16)[:, None] < jnp.arange(16)[None, :]
    starts = jnp.sum(jnp.where(before, lens[:, None], 0), axis=0)
    owned = owners[None, :] == targets[:, None]
    start = jnp.sum(jnp.where(owned, starts[None, :], 0), axis=1)
    size = jnp.sum(jnp.where(owned, lens[None, :], 0), axis=1)
    slot = jnp.arange(CAP)
    row = jnp.where(slot[None, :] < size[:, None], start[:, None] + slot[None, :], -1)
    return (row.reshape(-1)[:, None] == jnp.arange(TOK)[None, :]).astype(bf16)


def body(queries, keys, values, outputs, out_grads, lengths, owners):
    y, z = lax.axis_index("y"), lax.axis_index("zl")
    x, c, zh = lax.axis_index("x"), lax.axis_index("c"), lax.axis_index("zh")
    at = jnp.stack([y, z, x, c, zh]).astype(jnp.int32)

    def shift(a, axis, by):
        size = lax.axis_size(axis)
        return lax.ppermute(a, axis, [(i, (i + by) % size) for i in range(size)])

    kv = call(split_kv, 2, [shaped(KV_ROWS, HD)] * 4)(at, keys[0], values[0])
    kv_own = jnp.concatenate([kv[0]] + [shift(kv[k], "y", k) for k in (1, 2, 3)], axis=0)
    kv_all = [kv_own] + [
        lax.ppermute(kv_own, "zl", [(i, i + d) for i in range(4 - d)]) for d in (1, 2, 3)
    ]
    qd = call(split_qd, 3, [shaped(QD_ROWS, HD)] * 4)(at, queries[0], outputs[0], out_grads[0])
    qd_all = [qd[0]] + [shift(qd[k], "y", k) for k in (1, 2, 3)]

    meta = jnp.stack([lengths[0, 0], owners[0, 0]])
    other = shift(meta, "zh", 1)
    near = jnp.arange(8) // 2
    targets = zh * 8 + lax.rem(x + near, 4) * 2 + lax.rem(c + jnp.arange(8) % 2, 2)
    sel = jnp.stack([selection(meta[0], meta[1], targets), selection(other[0], other[1], targets)])

    grads = call(
        attention_grads,
        8,
        [shaped(QROWS, HD)] * 4 + [shaped(4 * KV_ROWS, HD)] * 4,
        [
            pltpu.VMEM((SLOTS, QD_ROWS, HD), bf16),
            pltpu.VMEM((4, BLK, HD), bf16),
            pltpu.VMEM((4, BLK, HD), bf16),
            pltpu.VMEM((4, BLK, QROWS), f32),
            pltpu.VMEM((4, BLK, HD), f32),
            pltpu.VMEM((4, BLK, HD), f32),
            pltpu.VMEM((SLOTS, QROWS, HD), bf16),
        ],
    )(at, *qd_all, *kv_all)
    dq, dkv = grads[:4], grads[4:]

    dq_back = [dq[0]] + [shift(dq[k], "y", 4 - k) for k in (1, 2, 3)]
    dq_far = [shift(a, "zh", 1) for a in dq_back]
    dkv_parts = [dkv[0]] + [
        lax.ppermute(dkv[d], "zl", [(i, i - d) for i in range(d, 4)]) for d in (1, 2, 3)
    ]
    dkv_sum = sum(a.astype(f32) for a in dkv_parts).astype(bf16)
    dkv_slots = [dkv_sum[k * KV_ROWS : (k + 1) * KV_ROWS] for k in range(4)]
    dkv_back = jnp.concatenate(
        [dkv_slots[0]] + [shift(dkv_slots[k], "y", 4 - k) for k in (1, 2, 3)], axis=0
    )
    dkv_far = shift(dkv_back, "zh", 1)

    def spread(pieces):
        out = []
        for kx in range(4):
            for cc in range(2):
                piece = pieces[kx * 2 + cc]
                if kx or cc:
                    pairs = [
                        (i, ((i // 2 + kx) % 4) * 2 + (i % 2 + cc) % 2) for i in range(8)
                    ]
                    piece = lax.ppermute(piece, ("x", "c"), pairs)
                out.append(piece)
        return out

    query_out = spread(
        call(pack_query, 9, [shaped(2, CAP, QH * HD)] * 8)(at, sel, *dq_back, *dq_far)
    )
    kv_out = spread(call(pack_kv, 3, [shaped(2, CAP, 2 * KVH * HD)] * 8)(at, sel, dkv_back, dkv_far))
    returned = call(
        place,
        16,
        shaped(16, CAP, (QH + 2 * KVH) * HD),
        [pltpu.SemaphoreType.DMA((32,))],
        pl.BlockSpec(memory_space=pl.ANY),
    )(at, *query_out, *kv_out)
    return returned[None, None]


def solution(mesh):
    split = Mesh(mesh.devices.reshape(2, 4, 2, 4, 4), ("zh", "x", "c", "zl", "y"))
    rows = P(("zh", "x", "c"), ("zl", "y"), None)
    return jax.shard_map(
        body,
        mesh=split,
        in_specs=(rows,) * 7,
        out_specs=P(("zh", "x", "c"), ("zl", "y"), None, None, None),
        check_vma=False,
    )
```

```python
import functools

import jax
import jax.numpy as jnp
from jax import lax
from jax.experimental import pallas as pl
from jax.experimental.pallas import tpu as pltpu
from jax.sharding import Mesh, PartitionSpec as P

HD = 128
QH = 16
KVH = 4
GROUP = QH // KVH
TOK = 128
CAP = 16
SLOTS = 4
BLK = SLOTS * TOK
QROWS = GROUP * TOK
QD_ROWS = 2 * QROWS + 16
KV_ROWS = 2 * TOK
FACTOR = HD ** (-0.5)
LOG2E = 1.4426950408889634
f32 = jnp.float32
bf16 = jnp.bfloat16
VMEM = pl.BlockSpec(memory_space=pltpu.VMEM)
SMEM = pl.BlockSpec(memory_space=pltpu.SMEM)
SMALL, LARGE = 12 * 2**20, 28 * 2**20


def aligned(index, unit):
    return pl.ds(pl.multiple_of(index * unit, unit), unit)


def split_kv(at_ref, k_ref, v_ref, *outs):
    y = at_ref[0]
    for slot in range(SLOTS):
        head = aligned(lax.rem(y + slot, SLOTS), HD)
        outs[slot][:TOK, :] = k_ref[:, head]
        outs[slot][TOK:, :] = v_ref[:, head]


def split_qd(at_ref, q_ref, o_ref, g_ref, after_ref, *outs):
    y = at_ref[0]
    lane = lax.broadcasted_iota(jnp.int32, (TOK, HD), 1)
    for slot in range(SLOTS):
        dest = lax.rem(y + slot, SLOTS)
        terms = jnp.zeros((TOK, HD), f32)
        for h in range(GROUP):
            head = aligned(dest * GROUP + h, HD)
            grad = g_ref[:, head]
            outs[slot][h * TOK : (h + 1) * TOK, :] = q_ref[:, head]
            outs[slot][QROWS + h * TOK : QROWS + (h + 1) * TOK, :] = grad
            term = jnp.sum(
                grad.astype(f32) * o_ref[:, head].astype(f32), axis=1, keepdims=True
            )
            terms = jnp.where(lax.rem(lane, GROUP) == h, term, terms)
        high = terms.astype(bf16).astype(f32)
        mid = (terms - high).astype(bf16).astype(f32)
        low = terms - high - mid
        part = lane // GROUP
        packed = jnp.where(
            part == 0, high, jnp.where(part == 1, mid, jnp.where(part == 2, low, 0.0))
        )
        outs[slot][2 * QROWS :, :] = packed.T[:16, :].astype(bf16)


def dot(a, b, dims):
    return lax.dot_general(a, b, (dims, ((), ())), preferred_element_type=f32)


def attention_grads(at_ref, *refs):
    qd_refs, kv_refs = refs[:4], refs[4:8]
    dq_refs, dkv_refs = refs[8:12], refs[12:16]
    qd, kk, vv, kacc, vacc, dqs, delta = refs[16:]
    y, z = at_ref[0], at_ref[1]
    natural = [lax.rem(y + SLOTS - s, SLOTS) for s in range(SLOTS)]
    for s in range(SLOTS):
        qd[natural[s]] = qd_refs[s][...]
    key_at = lax.broadcasted_iota(jnp.int32, (TOK, QROWS), 0)
    query_at = lax.rem(lax.broadcasted_iota(jnp.int32, (TOK, QROWS), 1), TOK)
    delta[...] = key_at - query_at

    def tile(blocks, part):
        query = qd[part, :QROWS, :]
        grad = qd[part, QROWS : 2 * QROWS, :]
        terms3 = qd[part, 2 * QROWS :, :].astype(f32)
        term4 = terms3[0:4] + terms3[4:8] + terms3[8:12]
        term = jnp.concatenate([term4[h : h + 1] for h in range(GROUP)], axis=1)
        scores, tops = [], []
        for d in range(blocks):
            score = dot(kk[d], query, ((1,), (1,)))
            if d == 0:
                score = jnp.concatenate(
                    [
                        jnp.where(
                            delta[...] <= (part - other) * TOK,
                            score[other * TOK : (other + 1) * TOK],
                            -jnp.inf,
                        )
                        for other in range(SLOTS)
                    ],
                    axis=0,
                )
            scores.append(score)
            tops.append(jnp.max(score, axis=0, keepdims=True))
        top = functools.reduce(jnp.maximum, tops)
        weights = [jnp.exp2((score - top) * (FACTOR * LOG2E)) for score in scores]
        inverse = 1.0 / sum(jnp.sum(weight, axis=0, keepdims=True) for weight in weights)
        dq = jnp.zeros((QROWS, HD), f32)
        for d in range(blocks):
            attn = weights[d] * inverse
            grad_attn = dot(vv[d], grad, ((1,), (1,)))
            low = (attn * (grad_attn - term)).astype(bf16)
            vacc[d] += dot(attn.astype(bf16), grad, ((1,), (0,)))
            kacc[d] += dot(low, query, ((1,), (0,)))
            dq = dq + dot(low, kk[d], ((0,), (0,)))
        dqs[part] = (dq * FACTOR).astype(bf16)

    def case(blocks):
        for d in range(blocks):
            for s in range(SLOTS):
                rows = aligned(natural[s], TOK)
                kk[d, rows, :] = kv_refs[d][s * KV_ROWS : s * KV_ROWS + TOK, :]
                vv[d, rows, :] = kv_refs[d][s * KV_ROWS + TOK : (s + 1) * KV_ROWS, :]
            kacc[d] = jnp.zeros((BLK, HD), f32)
            vacc[d] = jnp.zeros((BLK, HD), f32)

        def step(part, carry):
            tile(blocks, part)
            return carry

        lax.fori_loop(0, SLOTS, step, 0)
        for d in range(blocks):
            for s in range(SLOTS):
                rows = aligned(natural[s], TOK)
                dkv_refs[d][s * KV_ROWS : s * KV_ROWS + TOK, :] = (kacc[d, rows, :] * FACTOR).astype(bf16)
                dkv_refs[d][s * KV_ROWS + TOK : (s + 1) * KV_ROWS, :] = vacc[d, rows, :].astype(bf16)

    for ahead in range(4):
        pl.when(z == ahead)(functools.partial(case, ahead + 1))
    for s in range(SLOTS):
        dq_refs[s][...] = dqs[natural[s]]


def sum_kv(at_ref, own_ref, later_ref, *outs):
    total = (own_ref[...].astype(f32) + later_ref[...].astype(f32)).astype(bf16)
    for s in range(SLOTS):
        outs[s][...] = total[s * KV_ROWS : (s + 1) * KV_ROWS]


def pack(heads_of, at_ref, sel_ref, *refs):
    y = at_ref[0]
    parts, near, far = refs[:8], refs[8:12], refs[12:16]
    for doc in range(2):
        sel = sel_ref[doc]
        for slot in range(SLOTS):
            for row, place_of in heads_of(lax.rem(y + slot, SLOTS)):
                rows = parts[doc * SLOTS + slot][row : row + TOK, :]
                picked = dot(sel, rows, ((1,), (0,))).astype(bf16)
                for kx in range(4):
                    for outs, half in ((near, 0), (far, 1)):
                        first = (kx * 2 + half) * CAP
                        outs[kx][doc, :, aligned(place_of, HD)] = picked[first : first + CAP]


def query_heads(group):
    return [(h * TOK, group * GROUP + h) for h in range(GROUP)]


def kv_heads(group):
    return [(0, group), (TOK, KVH + group)]


def put(at_ref, pieces, out, sem, dz, columns):
    x, c, zh = at_ref[2], at_ref[3], at_ref[4]
    copies = []
    for kx in range(4):
        for cc in range(2):
            doc = lax.rem(zh + dz, 2) * 8 + lax.rem(x + 4 - kx, 4) * 2 + lax.rem(c + cc, 2)
            copies.append(
                pltpu.make_async_copy(
                    pieces[kx].at[cc], out.at[doc, :, columns], sem.at[kx * 2 + cc]
                )
            )
    return copies


QUERY_COLS = pl.ds(0, QH * HD)
KV_COLS = pl.ds(QH * HD, 2 * KVH * HD)


def place_first(at_ref, *refs):
    queries, kvs, query_far, out, sem = refs[:4], refs[4:8], refs[8], refs[9], refs[10]
    copies = put(at_ref, queries, out, sem.at[0], 0, QUERY_COLS)
    copies += put(at_ref, kvs, out, sem.at[1], 0, KV_COLS)
    copies += put(at_ref, [query_far.at[k] for k in range(4)], out, sem.at[2], 1, QUERY_COLS)
    for copy in copies:
        copy.start()
    for copy in copies:
        copy.wait()


def place_last(at_ref, kv_far, before, out, sem):
    copies = put(at_ref, [kv_far.at[k] for k in range(4)], out, sem, 1, KV_COLS)
    for copy in copies:
        copy.start()
    for copy in copies:
        copy.wait()


ANY = pl.BlockSpec(memory_space=pl.ANY)


def call(kernel, ins, outs, scratch=(), out_specs=None, aliases=None, limit=SMALL):
    return pl.pallas_call(
        kernel,
        out_shape=outs,
        in_specs=[SMEM] + ([VMEM] * ins if isinstance(ins, int) else ins),
        out_specs=out_specs or [VMEM] * len(outs),
        scratch_shapes=list(scratch),
        input_output_aliases=aliases or {},
        compiler_params=pltpu.CompilerParams(vmem_limit_bytes=limit),
    )


def shaped(*shape, dtype=bf16):
    return jax.ShapeDtypeStruct(shape, dtype)


def selection(lens, owners, targets):
    before = jnp.arange(16)[:, None] < jnp.arange(16)[None, :]
    starts = jnp.sum(jnp.where(before, lens[:, None], 0), axis=0)
    owned = owners[None, :] == targets[:, None]
    start = jnp.sum(jnp.where(owned, starts[None, :], 0), axis=1)
    size = jnp.sum(jnp.where(owned, lens[None, :], 0), axis=1)
    slot = jnp.arange(CAP)
    row = jnp.where(slot[None, :] < size[:, None], start[:, None] + slot[None, :], -1)
    return (row.reshape(-1)[:, None] == jnp.arange(TOK)[None, :]).astype(bf16)


def body(queries, keys, values, outputs, out_grads, lengths, owners):
    y, z = lax.axis_index("y"), lax.axis_index("zl")
    x, c, zh = lax.axis_index("x"), lax.axis_index("c"), lax.axis_index("zh")
    at = jnp.stack([y, z, x, c, zh]).astype(jnp.int32)

    def shift(a, axis, by):
        size = lax.axis_size(axis)
        return lax.ppermute(a, axis, [(i, (i + by) % size) for i in range(size)])

    kv = call(split_kv, 2, [shaped(KV_ROWS, HD)] * 4)(at, keys[0], values[0])
    kv_own = jnp.concatenate([kv[0]] + [shift(kv[k], "y", k) for k in (1, 2, 3)], axis=0)
    kv_all = [kv_own]
    for d in (1, 2, 3):
        kv_all.append(lax.ppermute(kv_all[-1], "zl", [(i, i + 1) for i in range(d - 1, 3)]))
    qd = call(split_qd, [VMEM] * 3 + [ANY], [shaped(QD_ROWS, HD)] * 4)(
        at, queries[0], outputs[0], out_grads[0], kv_own
    )
    qd_all = [qd[0]] + [shift(qd[k], "y", k) for k in (1, 2, 3)]

    meta = jnp.stack([lengths[0, 0], owners[0, 0]])
    meta, *qd_all = lax.optimization_barrier((meta, *qd_all))
    other = shift(meta, "c", 1)
    near = jnp.arange(8)
    targets = lax.rem(zh + near % 2, 2) * 8 + lax.rem(x + near // 2, 4) * 2 + c
    sel = jnp.stack([selection(meta[0], meta[1], targets), selection(other[0], other[1], targets)])

    grads = call(
        attention_grads,
        8,
        [shaped(QROWS, HD)] * 4 + [shaped(4 * KV_ROWS, HD)] * 4,
        [
            pltpu.VMEM((SLOTS, QD_ROWS, HD), bf16),
            pltpu.VMEM((4, BLK, HD), bf16),
            pltpu.VMEM((4, BLK, HD), bf16),
            pltpu.VMEM((4, BLK, HD), f32),
            pltpu.VMEM((4, BLK, HD), f32),
            pltpu.VMEM((SLOTS, QROWS, HD), bf16),
            pltpu.VMEM((TOK, QROWS), jnp.int32),
        ],
        limit=LARGE,
    )(at, *qd_all, *kv_all)
    dq, dkv = grads[:4], grads[4:]
    dkv_part = lax.ppermute(dkv[3], "zl", [(3, 2)])
    for d in (2, 1):
        dkv_part = (dkv[d].astype(f32) + dkv_part.astype(f32)).astype(bf16)
        dkv_part = lax.ppermute(dkv_part, "zl", [(i, i - 1) for i in range(d, 4)])

    def along_x(pieces):
        return [pieces[0]] + [shift(pieces[k], "x", k) for k in (1, 2, 3)]

    def packed(heads_of, parts, others, columns):
        out = call(
            functools.partial(pack, heads_of), 9, [shaped(2, CAP, columns)] * 8
        )(at, sel, *parts, *others)
        return out[:4], out[4:]

    dq_back = [dq[0]] + [shift(dq[k], "y", 4 - k) for k in (1, 2, 3)]
    dq_other = [shift(a, "c", 1) for a in dq_back]
    q_near, q_far = packed(query_heads, dq_back, dq_other, QH * HD)
    q_far = jnp.stack(along_x(q_far))
    q_far_in = shift(q_far, "zh", 1)
    q_near = along_x(q_near)

    slots = call(sum_kv, 2, [shaped(KV_ROWS, HD)] * 4)(at, dkv[0], dkv_part)
    dkv_back = [slots[0]] + [shift(slots[k], "y", 4 - k) for k in (1, 2, 3)]
    dkv_other = [shift(a, "c", 1) for a in dkv_back]
    kv_near, kv_far = packed(kv_heads, dkv_back, dkv_other, 2 * KVH * HD)
    kv_far = jnp.stack(along_x(kv_far))
    kv_far_in = shift(kv_far, "zh", 1)
    kv_near = along_x(kv_near)

    whole = shaped(16, CAP, (QH + 2 * KVH) * HD)
    returned = call(
        place_first, 9, whole, [pltpu.SemaphoreType.DMA((3, 8))], ANY
    )(at, *q_near, *kv_near, q_far_in)
    returned = call(
        place_last, [VMEM, ANY], whole, [pltpu.SemaphoreType.DMA((8,))], ANY, {2: 0}
    )(at, kv_far_in, returned)
    return returned[None, None]


def solution(mesh):
    split = Mesh(mesh.devices.reshape(2, 4, 2, 4, 4), ("zh", "x", "c", "zl", "y"))
    rows = P(("zh", "x", "c"), ("zl", "y"), None)
    return jax.shard_map(
        body,
        mesh=split,
        in_specs=(rows,) * 7,
        out_specs=P(("zh", "x", "c"), ("zl", "y"), None, None, None),
        check_vma=False,
    )
```

```python
import functools

import jax
import jax.numpy as jnp
from jax import lax
from jax.experimental import pallas as pl
from jax.experimental.pallas import tpu as pltpu
from jax.sharding import Mesh, PartitionSpec as P

HD = 128
QH = 16
KVH = 4
GROUP = QH // KVH
TOK = 128
CAP = 16
DOCS = 16
SLOTS = 4
BLK = SLOTS * TOK
QROWS = GROUP * TOK
QD_ROWS = 2 * QROWS + 16
KV_ROWS = 2 * TOK
FACTOR = HD ** (-0.5)
LOG2E = 1.4426950408889634
f32 = jnp.float32
bf16 = jnp.bfloat16
VMEM = pl.BlockSpec(memory_space=pltpu.VMEM)
SMEM = pl.BlockSpec(memory_space=pltpu.SMEM)
SMALL, LARGE, WHOLE = 12 * 2**20, 28 * 2**20, 56 * 2**20


def aligned(index, unit):
    return pl.ds(pl.multiple_of(index * unit, unit), unit)


def split_kv(at_ref, k_ref, v_ref, *outs):
    z = at_ref[1]
    for slot in range(SLOTS):
        head = aligned(lax.rem(z + slot, SLOTS), HD)
        outs[slot][:TOK, :] = k_ref[:, head]
        outs[slot][TOK:, :] = v_ref[:, head]


def split_qd(at_ref, q_ref, o_ref, g_ref, after_ref, *outs):
    z = at_ref[1]
    lane = lax.broadcasted_iota(jnp.int32, (TOK, HD), 1)
    for slot in range(SLOTS):
        dest = lax.rem(z + slot, SLOTS)
        terms = jnp.zeros((TOK, HD), f32)
        for h in range(GROUP):
            head = aligned(dest * GROUP + h, HD)
            grad = g_ref[:, head]
            outs[slot][h * TOK : (h + 1) * TOK, :] = q_ref[:, head]
            outs[slot][QROWS + h * TOK : QROWS + (h + 1) * TOK, :] = grad
            term = jnp.sum(
                grad.astype(f32) * o_ref[:, head].astype(f32), axis=1, keepdims=True
            )
            terms = jnp.where(lax.rem(lane, GROUP) == h, term, terms)
        high = terms.astype(bf16).astype(f32)
        mid = (terms - high).astype(bf16).astype(f32)
        low = terms - high - mid
        part = lane // GROUP
        packed = jnp.where(
            part == 0, high, jnp.where(part == 1, mid, jnp.where(part == 2, low, 0.0))
        )
        outs[slot][2 * QROWS :, :] = packed.T[:16, :].astype(bf16)


def dot(a, b, dims):
    return lax.dot_general(a, b, (dims, ((), ())), preferred_element_type=f32)


def attention_grads(at_ref, *refs):
    kv_refs, qd_refs = refs[:4], refs[4:8]
    dq_refs, dkv_refs = refs[8:12], refs[12:16]
    qd, kk, vv, kacc, vacc, dqs, delta = refs[16:]
    y, z = at_ref[0], at_ref[1]
    along_z = [lax.rem(z + SLOTS - s, SLOTS) for s in range(SLOTS)]
    along_y = [aligned(lax.rem(y + SLOTS - k, SLOTS), TOK) for k in range(4)]
    for s in range(SLOTS):
        qd[along_z[s]] = qd_refs[s][...]
        for k in range(4):
            kk[along_z[s], along_y[k], :] = kv_refs[k][s * KV_ROWS : s * KV_ROWS + TOK, :]
            vv[along_z[s], along_y[k], :] = kv_refs[k][s * KV_ROWS + TOK : (s + 1) * KV_ROWS, :]
    key_at = lax.broadcasted_iota(jnp.int32, (TOK, QROWS), 0)
    query_at = lax.rem(lax.broadcasted_iota(jnp.int32, (TOK, QROWS), 1), TOK)
    delta[...] = key_at - query_at

    for part in range(SLOTS):
        query = qd[part, :QROWS, :]
        grad = qd[part, QROWS : 2 * QROWS, :]
        terms3 = qd[part, 2 * QROWS :, :].astype(f32)
        term4 = terms3[0:4] + terms3[4:8] + terms3[8:12]
        term = jnp.concatenate([term4[h : h + 1] for h in range(GROUP)], axis=1)
        scores = [dot(kk[t], query, ((1,), (1,))) for t in range(part + 1)]
        scores[part] = jnp.concatenate(
            [
                jnp.where(
                    delta[...] <= (y - other) * TOK,
                    scores[part][other * TOK : (other + 1) * TOK],
                    -jnp.inf,
                )
                for other in range(SLOTS)
            ],
            axis=0,
        )
        top = functools.reduce(
            jnp.maximum, [jnp.max(score, axis=0, keepdims=True) for score in scores]
        )
        weights = [jnp.exp2((score - top) * (FACTOR * LOG2E)) for score in scores]
        inverse = 1.0 / sum(jnp.sum(weight, axis=0, keepdims=True) for weight in weights)
        dq = jnp.zeros((QROWS, HD), f32)
        for t in range(part + 1):
            attn = weights[t] * inverse
            grad_attn = dot(vv[t], grad, ((1,), (1,)))
            low = (attn * (grad_attn - term)).astype(bf16)
            value_part = dot(attn.astype(bf16), grad, ((1,), (0,)))
            key_part = dot(low, query, ((1,), (0,)))
            if t == part:
                vacc[t] = value_part
                kacc[t] = key_part
            else:
                vacc[t] += value_part
                kacc[t] += key_part
            dq = dq + dot(low, kk[t], ((0,), (0,)))
        dqs[part] = (dq * FACTOR).astype(bf16)

    for s in range(SLOTS):
        dq_refs[s][...] = dqs[along_z[s]]
        for k in range(4):
            keys = kacc[along_z[s], along_y[k], :]
            dkv_refs[k][s * KV_ROWS : s * KV_ROWS + TOK, :] = (keys * FACTOR).astype(bf16)
            values = vacc[along_z[s], along_y[k], :]
            dkv_refs[k][s * KV_ROWS + TOK : (s + 1) * KV_ROWS, :] = values.astype(bf16)


def sum_kv(at_ref, own_ref, one_ref, two_ref, three_ref, *outs):
    total = own_ref[...].astype(f32) + one_ref[...].astype(f32)
    total = (total + two_ref[...].astype(f32) + three_ref[...].astype(f32)).astype(bf16)
    for s in range(SLOTS):
        outs[s][...] = total[s * KV_ROWS : (s + 1) * KV_ROWS]


def pack(at_ref, sel_ref, *refs):
    z = at_ref[1]
    queries, kvs, out = refs[:4], refs[4:8], refs[8]
    sel = sel_ref[...]

    def put(rows, place_of):
        picked = dot(sel, rows, ((1,), (0,))).astype(bf16)
        out[:, :, aligned(place_of, HD)] = picked.reshape(DOCS, CAP, HD)

    for slot in range(SLOTS):
        group = lax.rem(z + slot, SLOTS)
        for h in range(GROUP):
            put(queries[slot][h * TOK : (h + 1) * TOK, :], group * GROUP + h)
        put(kvs[slot][:TOK, :], QH + group)
        put(kvs[slot][TOK:, :], QH + KVH + group)


ANY = pl.BlockSpec(memory_space=pl.ANY)


def call(kernel, ins, outs, scratch=(), out_specs=None, aliases=None, limit=SMALL):
    return pl.pallas_call(
        kernel,
        out_shape=outs,
        in_specs=[SMEM] + ([VMEM] * ins if isinstance(ins, int) else ins),
        out_specs=out_specs or [VMEM] * len(outs),
        scratch_shapes=list(scratch),
        input_output_aliases=aliases or {},
        compiler_params=pltpu.CompilerParams(vmem_limit_bytes=limit),
    )


def shaped(*shape, dtype=bf16):
    return jax.ShapeDtypeStruct(shape, dtype)


def selection(lens, owners, targets):
    before = jnp.arange(16)[:, None] < jnp.arange(16)[None, :]
    starts = jnp.sum(jnp.where(before, lens[:, None], 0), axis=0)
    owned = owners[None, :] == targets[:, None]
    start = jnp.sum(jnp.where(owned, starts[None, :], 0), axis=1)
    size = jnp.sum(jnp.where(owned, lens[None, :], 0), axis=1)
    slot = jnp.arange(CAP)
    row = jnp.where(slot[None, :] < size[:, None], start[:, None] + slot[None, :], -1)
    return (row.reshape(-1)[:, None] == jnp.arange(TOK)[None, :]).astype(bf16)


def body(queries, keys, values, outputs, out_grads, lengths, owners):
    y, z = lax.axis_index("y"), lax.axis_index("zl")
    at = jnp.stack([y, z]).astype(jnp.int32)

    def shift(a, axis, by):
        size = lax.axis_size(axis)
        return lax.ppermute(a, axis, [(i, (i + by) % size) for i in range(size)])

    kv = call(split_kv, 2, [shaped(KV_ROWS, HD)] * 4, limit=WHOLE)(at, keys[0], values[0])
    kv_own = jnp.concatenate([kv[0]] + [shift(kv[k], "zl", k) for k in (1, 2, 3)], axis=0)
    kv_all = [kv_own] + [shift(kv_own, "y", k) for k in (1, 2, 3)]
    qd = call(split_qd, [VMEM] * 3 + [ANY], [shaped(QD_ROWS, HD)] * 4, limit=WHOLE)(
        at, queries[0], outputs[0], out_grads[0], kv[1]
    )
    qd_all = [qd[0]] + [shift(qd[k], "zl", k) for k in (1, 2, 3)]

    sel = selection(lengths[0, 0], owners[0, 0], jnp.arange(DOCS))

    grads = call(
        attention_grads,
        8,
        [shaped(QROWS, HD)] * 4 + [shaped(4 * KV_ROWS, HD)] * 4,
        [
            pltpu.VMEM((SLOTS, QD_ROWS, HD), bf16),
            pltpu.VMEM((4, BLK, HD), bf16),
            pltpu.VMEM((4, BLK, HD), bf16),
            pltpu.VMEM((4, BLK, HD), f32),
            pltpu.VMEM((4, BLK, HD), f32),
            pltpu.VMEM((SLOTS, QROWS, HD), bf16),
            pltpu.VMEM((TOK, QROWS), jnp.int32),
        ],
        limit=LARGE,
    )(at, *kv_all, *qd_all)
    dq, dkv = grads[:4], grads[4:]
    dkv_parts = [dkv[0]] + [shift(dkv[k], "y", 4 - k) for k in (1, 2, 3)]

    dq_back = [dq[0]] + [shift(dq[k], "zl", 4 - k) for k in (1, 2, 3)]
    slots = call(sum_kv, 4, [shaped(KV_ROWS, HD)] * 4)(at, *dkv_parts)
    dkv_back = [slots[0]] + [shift(slots[k], "zl", 4 - k) for k in (1, 2, 3)]
    rows = call(pack, 9, shaped(DOCS, CAP, (QH + 2 * KVH) * HD), out_specs=VMEM)(
        at, sel, *dq_back, *dkv_back
    )
    returned = lax.all_to_all(rows, ("zh", "x", "c"), 0, 0, tiled=True)
    return returned[None, None]


def solution(mesh):
    split = Mesh(mesh.devices.reshape(2, 4, 2, 4, 4), ("zh", "x", "c", "zl", "y"))
    rows = P(("zh", "x", "c"), ("zl", "y"), None)
    return jax.shard_map(
        body,
        mesh=split,
        in_specs=(rows,) * 7,
        out_specs=P(("zh", "x", "c"), ("zl", "y"), None, None, None),
        check_vma=False,
    )
```

```python
import functools

import jax
import jax.numpy as jnp
from jax import lax
from jax.experimental import pallas as pl
from jax.experimental.pallas import tpu as pltpu
from jax.sharding import Mesh, PartitionSpec as P

HD = 128
QH = 16
KVH = 4
GROUP = QH // KVH
TOK = 128
CAP = 16
DOCS = 16
CODE_ROW = 12
SLOTS = 4
BLK = SLOTS * TOK
QROWS = GROUP * TOK
QD_ROWS = 2 * QROWS + 16
KV_ROWS = 2 * TOK
FACTOR = HD ** (-0.5)
LOG2E = 1.4426950408889634
f32 = jnp.float32
bf16 = jnp.bfloat16
VMEM = pl.BlockSpec(memory_space=pltpu.VMEM)
SMEM = pl.BlockSpec(memory_space=pltpu.SMEM)
SMALL, LARGE, WHOLE = 12 * 2**20, 20 * 2**20, 56 * 2**20


def aligned(index, unit):
    return pl.ds(pl.multiple_of(index * unit, unit), unit)


def split_kv(at_ref, k_ref, v_ref, *outs):
    z = at_ref[1]
    for slot in range(SLOTS):
        head = aligned(lax.rem(z + slot, SLOTS), HD)
        outs[slot][:TOK, :] = k_ref[:, head]
        outs[slot][TOK:, :] = v_ref[:, head]


def split_qd(at_ref, lens_ref, owners_ref, q_ref, o_ref, g_ref, after_ref, *outs):
    z = at_ref[1]
    lane = lax.broadcasted_iota(jnp.int32, (TOK, HD), 1)
    position = lax.broadcasted_iota(jnp.int32, (16, TOK), 1)
    code = jnp.zeros((16, TOK), jnp.int32)
    start = 0
    for child in range(16):
        code = jnp.where(position >= start, owners_ref[child] * CAP + position - start, code)
        start = start + lens_ref[child]
    row = lax.broadcasted_iota(jnp.int32, (16, TOK), 0)
    code = jnp.where(row == CODE_ROW, code, 0).astype(f32)
    for slot in range(SLOTS):
        dest = lax.rem(z + slot, SLOTS)
        terms = jnp.zeros((TOK, HD), f32)
        for h in range(GROUP):
            head = aligned(dest * GROUP + h, HD)
            grad = g_ref[:, head]
            outs[slot][h * TOK : (h + 1) * TOK, :] = q_ref[:, head]
            outs[slot][QROWS + h * TOK : QROWS + (h + 1) * TOK, :] = grad
            term = jnp.sum(
                grad.astype(f32) * o_ref[:, head].astype(f32), axis=1, keepdims=True
            )
            terms = jnp.where(lax.rem(lane, GROUP) == h, term, terms)
        high = terms.astype(bf16).astype(f32)
        mid = (terms - high).astype(bf16).astype(f32)
        low = terms - high - mid
        part = lane // GROUP
        packed = jnp.where(
            part == 0, high, jnp.where(part == 1, mid, jnp.where(part == 2, low, 0.0))
        )
        outs[slot][2 * QROWS :, :] = (packed.T[:16, :] + code).astype(bf16)


def dot(a, b, dims):
    return lax.dot_general(a, b, (dims, ((), ())), preferred_element_type=f32)


def attention_grads(at_ref, *refs):
    kv_refs, qd_refs = refs[:4], refs[4:8]
    dq_ref, code_ref, dkv_refs = refs[8], refs[9], refs[10:14]
    qd, kk, vv, kacc, vacc, delta = refs[14:]
    y, z = at_ref[0], at_ref[1]
    along_z = [lax.rem(z + SLOTS - s, SLOTS) for s in range(SLOTS)]
    along_y = [aligned(lax.rem(y + SLOTS - k, SLOTS), TOK) for k in range(4)]
    for s in range(SLOTS):
        qd[along_z[s]] = qd_refs[s][...]
        for k in range(4):
            kk[along_z[s], along_y[k], :] = kv_refs[k][s * KV_ROWS : s * KV_ROWS + TOK, :]
            vv[along_z[s], along_y[k], :] = kv_refs[k][s * KV_ROWS + TOK : (s + 1) * KV_ROWS, :]
    key_at = lax.broadcasted_iota(jnp.int32, (TOK, QROWS), 0)
    query_at = lax.rem(lax.broadcasted_iota(jnp.int32, (TOK, QROWS), 1), TOK)
    delta[...] = key_at - query_at

    for part in range(SLOTS):
        query = qd[part, :QROWS, :]
        grad = qd[part, QROWS : 2 * QROWS, :]
        terms3 = qd[part, 2 * QROWS :, :].astype(f32)
        term4 = terms3[0:4] + terms3[4:8] + terms3[8:12]
        term = jnp.concatenate([term4[h : h + 1] for h in range(GROUP)], axis=1)
        scores = [dot(kk[t], query, ((1,), (1,))) for t in range(part + 1)]
        scores[part] = jnp.concatenate(
            [
                jnp.where(
                    delta[...] <= (y - other) * TOK,
                    scores[part][other * TOK : (other + 1) * TOK],
                    -jnp.inf,
                )
                for other in range(SLOTS)
            ],
            axis=0,
        )
        top = functools.reduce(
            jnp.maximum, [jnp.max(score, axis=0, keepdims=True) for score in scores]
        )
        weights = [jnp.exp2((score - top) * (FACTOR * LOG2E)) for score in scores]
        inverse = 1.0 / sum(jnp.sum(weight, axis=0, keepdims=True) for weight in weights)
        dq = jnp.zeros((QROWS, HD), f32)
        for t in range(part + 1):
            attn = weights[t] * inverse
            grad_attn = dot(vv[t], grad, ((1,), (1,)))
            low = (attn * (grad_attn - term)).astype(bf16)
            value_part = dot(attn.astype(bf16), grad, ((1,), (0,)))
            key_part = dot(low, query, ((1,), (0,)))
            if t == part:
                vacc[t] = value_part
                kacc[t] = key_part
            else:
                vacc[t] += value_part
                kacc[t] += key_part
            dq = dq + dot(low, kk[t], ((0,), (0,)))
        dq_ref[part] = (dq * FACTOR).astype(bf16)
        code_ref[part] = qd[part, 2 * QROWS :, :]

    for t in range(SLOTS):
        for k in range(4):
            keys = kacc[t, along_y[k], :]
            dkv_refs[k][t * KV_ROWS : t * KV_ROWS + TOK, :] = (keys * FACTOR).astype(bf16)
            values = vacc[t, along_y[k], :]
            dkv_refs[k][t * KV_ROWS + TOK : (t + 1) * KV_ROWS, :] = values.astype(bf16)


def pick(code_ref, t, heads, out_ref):
    slot_code = lax.broadcasted_iota(jnp.int32, (DOCS * CAP, TOK), 0)
    code = code_ref[t].astype(f32)[CODE_ROW : CODE_ROW + 1].astype(jnp.int32)
    sel = jnp.where(slot_code == code, 1.0, 0.0).astype(bf16)
    for place, rows in enumerate(heads):
        picked = dot(sel, rows, ((1,), (0,))).astype(bf16)
        out_ref[:, t, :, place * HD : (place + 1) * HD] = picked.reshape(DOCS, CAP, HD)


def pack_query(at_ref, dq_ref, code_ref, out_ref):
    for t in range(SLOTS):
        pick(code_ref, t, [dq_ref[t, h * TOK : (h + 1) * TOK, :] for h in range(GROUP)], out_ref)


def pack_kv(at_ref, code_ref, own_ref, one_ref, two_ref, three_ref, out_ref):
    total = own_ref[...].astype(f32) + one_ref[...].astype(f32)
    total = (total + two_ref[...].astype(f32) + three_ref[...].astype(f32)).astype(bf16)
    for t in range(SLOTS):
        first = t * KV_ROWS
        heads = [total[first : first + TOK], total[first + TOK : first + KV_ROWS]]
        pick(code_ref, t, heads, out_ref)


def place(at_ref, query_ref, kv_ref, out, sem):
    copies = []
    for group in range(SLOTS):
        for source, first, width, to in (
            (query_ref, 0, QROWS, group * GROUP * HD),
            (kv_ref, 0, HD, (QH + group) * HD),
            (kv_ref, HD, HD, (QH + KVH + group) * HD),
        ):
            copies.append(
                pltpu.make_async_copy(
                    source.at[:, group, :, pl.ds(first, width)],
                    out.at[:, :, pl.ds(to, width)],
                    sem.at[len(copies)],
                )
            )
    for copy in copies:
        copy.start()
    for copy in copies:
        copy.wait()


ANY = pl.BlockSpec(memory_space=pl.ANY)


def call(kernel, ins, outs, scratch=(), out_specs=None, aliases=None, limit=SMALL):
    return pl.pallas_call(
        kernel,
        out_shape=outs,
        in_specs=[SMEM] + ([VMEM] * ins if isinstance(ins, int) else ins),
        out_specs=out_specs or [VMEM] * len(outs),
        scratch_shapes=list(scratch),
        input_output_aliases=aliases or {},
        compiler_params=pltpu.CompilerParams(vmem_limit_bytes=limit),
    )


def shaped(*shape, dtype=bf16):
    return jax.ShapeDtypeStruct(shape, dtype)


def body(queries, keys, values, outputs, out_grads, lengths, owners):
    y, z = lax.axis_index("y"), lax.axis_index("zl")
    at = jnp.stack([y, z]).astype(jnp.int32)

    def shift(a, axis, by):
        size = lax.axis_size(axis)
        return lax.ppermute(a, axis, [(i, (i + by) % size) for i in range(size)])

    kv = call(split_kv, 2, [shaped(KV_ROWS, HD)] * 4, limit=WHOLE)(at, keys[0], values[0])
    kv_own = jnp.concatenate([kv[0]] + [shift(kv[k], "zl", k) for k in (1, 2, 3)], axis=0)
    kv_all = [kv_own] + [shift(kv_own, "y", k) for k in (1, 2, 3)]
    qd = call(split_qd, [SMEM] * 2 + [VMEM] * 3 + [ANY], [shaped(QD_ROWS, HD)] * 4, limit=WHOLE)(
        at, lengths[0, 0], owners[0, 0], queries[0], outputs[0], out_grads[0], kv[1]
    )
    qd_all = [qd[0]] + [shift(qd[k], "zl", k) for k in (1, 2, 3)]

    dq, codes, *dkv = call(
        attention_grads,
        8,
        [shaped(SLOTS, QROWS, HD), shaped(SLOTS, 16, HD)] + [shaped(4 * KV_ROWS, HD)] * 4,
        [
            pltpu.VMEM((SLOTS, QD_ROWS, HD), bf16),
            pltpu.VMEM((4, BLK, HD), bf16),
            pltpu.VMEM((4, BLK, HD), bf16),
            pltpu.VMEM((4, BLK, HD), f32),
            pltpu.VMEM((4, BLK, HD), f32),
            pltpu.VMEM((TOK, QROWS), jnp.int32),
        ],
        limit=LARGE,
    )(at, *kv_all, *qd_all)
    dkv_parts = [dkv[0]] + [shift(dkv[k], "y", 4 - k) for k in (1, 2, 3)]

    def to_owners(kernel, operands, heads):
        shape = (DOCS, SLOTS, CAP, heads * HD)
        rows = call(kernel, len(operands), shaped(*shape), out_specs=VMEM)(at, *operands)
        rows = rows.reshape(DOCS * SLOTS, CAP, heads * HD)
        rows = lax.all_to_all(rows, ("zh", "x", "c", "zl"), 0, 0, tiled=True)
        return rows.reshape(shape)

    query_rows = to_owners(pack_query, [dq, codes], GROUP)
    query_rows, *dkv_parts = lax.optimization_barrier((query_rows, *dkv_parts))
    kv_rows = to_owners(pack_kv, [codes, *dkv_parts], 2)
    returned = call(
        place,
        2,
        shaped(DOCS, CAP, (QH + 2 * KVH) * HD),
        [pltpu.SemaphoreType.DMA((3 * SLOTS,))],
        ANY,
    )(at, query_rows, kv_rows)
    return returned[None, None]


def solution(mesh):
    split = Mesh(mesh.devices.reshape(2, 4, 2, 4, 4), ("zh", "x", "c", "zl", "y"))
    rows = P(("zh", "x", "c"), ("zl", "y"), None)
    return jax.shard_map(
        body,
        mesh=split,
        in_specs=(rows,) * 7,
        out_specs=P(("zh", "x", "c"), ("zl", "y"), None, None, None),
        check_vma=False,
    )
```

```python
import functools

import jax
import jax.numpy as jnp
from jax import lax
from jax.experimental import pallas as pl
from jax.experimental.pallas import tpu as pltpu
from jax.sharding import Mesh, PartitionSpec as P

HD = 128
QH = 16
KVH = 4
GROUP = QH // KVH
TOK = 128
CAP = 16
DOCS = 16
CODE_ROW = 12
SLOTS = 4
BLK = SLOTS * TOK
QROWS = GROUP * TOK
QD_ROWS = 2 * QROWS + 16
KV_ROWS = 2 * TOK
FACTOR = HD ** (-0.5)
LOG2E = 1.4426950408889634
f32 = jnp.float32
bf16 = jnp.bfloat16
VMEM = pl.BlockSpec(memory_space=pltpu.VMEM)
SMEM = pl.BlockSpec(memory_space=pltpu.SMEM)
SMALL, LARGE, WHOLE = 12 * 2**20, 20 * 2**20, 56 * 2**20


def aligned(index, unit):
    return pl.ds(pl.multiple_of(index * unit, unit), unit)


def split_kv(k_ref, v_ref, *outs):
    z = lax.axis_index("zl")
    for slot in range(SLOTS):
        head = aligned(lax.rem(z + slot, SLOTS), HD)
        outs[slot][:TOK, :] = k_ref[:, head]
        outs[slot][TOK:, :] = v_ref[:, head]


def split_qd(lens_ref, owners_ref, q_ref, o_ref, g_ref, after_ref, *outs):
    z = lax.axis_index("zl")
    lane = lax.broadcasted_iota(jnp.int32, (TOK, HD), 1)
    position = lax.broadcasted_iota(jnp.int32, (16, TOK), 1)
    code = jnp.zeros((16, TOK), jnp.int32)
    start = 0
    for child in range(16):
        code = jnp.where(position >= start, owners_ref[child] * CAP + position - start, code)
        start = start + lens_ref[child]
    row = lax.broadcasted_iota(jnp.int32, (16, TOK), 0)
    code = jnp.where(row == CODE_ROW, code, 0).astype(f32)
    for slot in range(SLOTS):
        dest = lax.rem(z + slot, SLOTS)
        terms = jnp.zeros((TOK, HD), f32)
        for h in range(GROUP):
            head = aligned(dest * GROUP + h, HD)
            grad = g_ref[:, head]
            outs[slot][h * TOK : (h + 1) * TOK, :] = q_ref[:, head]
            outs[slot][QROWS + h * TOK : QROWS + (h + 1) * TOK, :] = grad
            term = jnp.sum(
                grad.astype(f32) * o_ref[:, head].astype(f32), axis=1, keepdims=True
            )
            terms = jnp.where(lax.rem(lane, GROUP) == h, term, terms)
        high = terms.astype(bf16).astype(f32)
        mid = (terms - high).astype(bf16).astype(f32)
        low = terms - high - mid
        part = lane // GROUP
        packed = jnp.where(
            part == 0, high, jnp.where(part == 1, mid, jnp.where(part == 2, low, 0.0))
        )
        outs[slot][2 * QROWS :, :] = (packed.T[:16, :] + code).astype(bf16)


def dot(a, b, dims):
    return lax.dot_general(a, b, (dims, ((), ())), preferred_element_type=f32)


def attention_grads(*refs):
    kv_refs, qd_refs = refs[:4], refs[4:8]
    dq_ref, code_ref, dkv_refs = refs[8], refs[9], refs[10:14]
    qd, kk, vv, kacc, vacc, delta = refs[14:]
    y, z = lax.axis_index("y"), lax.axis_index("zl")
    along_z = [lax.rem(z + SLOTS - s, SLOTS) for s in range(SLOTS)]
    along_y = [aligned(lax.rem(y + SLOTS - k, SLOTS), TOK) for k in range(4)]
    for s in range(SLOTS):
        qd[along_z[s]] = qd_refs[s][...]
        for k in range(4):
            kk[along_z[s], along_y[k], :] = kv_refs[k][s * KV_ROWS : s * KV_ROWS + TOK, :]
            vv[along_z[s], along_y[k], :] = kv_refs[k][s * KV_ROWS + TOK : (s + 1) * KV_ROWS, :]
    key_at = lax.broadcasted_iota(jnp.int32, (TOK, QROWS), 0)
    query_at = lax.rem(lax.broadcasted_iota(jnp.int32, (TOK, QROWS), 1), TOK)
    delta[...] = key_at - query_at

    for part in range(SLOTS):
        query = qd[part, :QROWS, :]
        grad = qd[part, QROWS : 2 * QROWS, :]
        terms3 = qd[part, 2 * QROWS :, :].astype(f32)
        term4 = terms3[0:4] + terms3[4:8] + terms3[8:12]
        term = jnp.concatenate([term4[h : h + 1] for h in range(GROUP)], axis=1)
        scores = [dot(kk[t], query, ((1,), (1,))) for t in range(part + 1)]
        scores[part] = jnp.concatenate(
            [
                jnp.where(
                    delta[...] <= (y - other) * TOK,
                    scores[part][other * TOK : (other + 1) * TOK],
                    -jnp.inf,
                )
                for other in range(SLOTS)
            ],
            axis=0,
        )
        top = functools.reduce(
            jnp.maximum, [jnp.max(score, axis=0, keepdims=True) for score in scores]
        )
        weights = [jnp.exp2((score - top) * (FACTOR * LOG2E)) for score in scores]
        inverse = 1.0 / sum(jnp.sum(weight, axis=0, keepdims=True) for weight in weights)
        dq = jnp.zeros((QROWS, HD), f32)
        for t in range(part + 1):
            attn = weights[t] * inverse
            grad_attn = dot(vv[t], grad, ((1,), (1,)))
            low = (attn * (grad_attn - term)).astype(bf16)
            value_part = dot(attn.astype(bf16), grad, ((1,), (0,)))
            key_part = dot(low, query, ((1,), (0,)))
            if t == part:
                vacc[t] = value_part
                kacc[t] = key_part
            else:
                vacc[t] += value_part
                kacc[t] += key_part
            dq = dq + dot(low, kk[t], ((0,), (0,)))
        dq_ref[part] = (dq * FACTOR).astype(bf16)
        code_ref[part] = qd[part, 2 * QROWS :, :]

    for t in range(SLOTS):
        for k in range(4):
            keys = kacc[t, along_y[k], :]
            dkv_refs[k][t * KV_ROWS : t * KV_ROWS + TOK, :] = (keys * FACTOR).astype(bf16)
            values = vacc[t, along_y[k], :]
            dkv_refs[k][t * KV_ROWS + TOK : (t + 1) * KV_ROWS, :] = values.astype(bf16)


def pick(code_ref, t, heads, out_ref):
    slot_code = lax.broadcasted_iota(jnp.int32, (DOCS * CAP, TOK), 0)
    code = code_ref[t].astype(f32)[CODE_ROW : CODE_ROW + 1].astype(jnp.int32)
    sel = jnp.where(slot_code == code, 1.0, 0.0).astype(bf16)
    for place, rows in enumerate(heads):
        picked = dot(sel, rows, ((1,), (0,))).astype(bf16)
        out_ref[:, t, :, place * HD : (place + 1) * HD] = picked.reshape(DOCS, CAP, HD)


def pack_query(dq_ref, code_ref, out_ref):
    for t in range(SLOTS):
        pick(code_ref, t, [dq_ref[t, h * TOK : (h + 1) * TOK, :] for h in range(GROUP)], out_ref)


def pack_kv(code_ref, own_ref, one_ref, two_ref, three_ref, out_ref):
    total = own_ref[...].astype(f32) + one_ref[...].astype(f32)
    total = (total + two_ref[...].astype(f32) + three_ref[...].astype(f32)).astype(bf16)
    for t in range(SLOTS):
        first = t * KV_ROWS
        heads = [total[first : first + TOK], total[first + TOK : first + KV_ROWS]]
        pick(code_ref, t, heads, out_ref)


def place(query_ref, kv_ref, out, sem):
    copies = []
    for group in range(SLOTS):
        for source, first, width, to in (
            (query_ref, 0, QROWS, group * GROUP * HD),
            (kv_ref, 0, HD, (QH + group) * HD),
            (kv_ref, HD, HD, (QH + KVH + group) * HD),
        ):
            copies.append(
                pltpu.make_async_copy(
                    source.at[:, group, :, pl.ds(first, width)],
                    out.at[:, :, pl.ds(to, width)],
                    sem.at[len(copies)],
                )
            )
    for copy in copies:
        copy.start()
    for copy in copies:
        copy.wait()


ANY = pl.BlockSpec(memory_space=pl.ANY)


def call(kernel, ins, outs, scratch=(), out_specs=None, aliases=None, limit=SMALL):
    return pl.pallas_call(
        kernel,
        out_shape=outs,
        in_specs=[VMEM] * ins if isinstance(ins, int) else ins,
        out_specs=out_specs or [VMEM] * len(outs),
        scratch_shapes=list(scratch),
        input_output_aliases=aliases or {},
        compiler_params=pltpu.CompilerParams(vmem_limit_bytes=limit),
    )


def shaped(*shape, dtype=bf16):
    return jax.ShapeDtypeStruct(shape, dtype)


def body(queries, keys, values, outputs, out_grads, lengths, owners):
    def shift(a, axis, by):
        size = lax.axis_size(axis)
        return lax.ppermute(a, axis, [(i, (i + by) % size) for i in range(size)])

    kv = call(split_kv, 2, [shaped(KV_ROWS, HD)] * 4, limit=WHOLE)(keys[0], values[0])
    kv_own = jnp.concatenate([kv[0]] + [shift(kv[k], "zl", k) for k in (1, 2, 3)], axis=0)
    kv_all = [kv_own] + [shift(kv_own, "y", k) for k in (1, 2, 3)]
    qd = call(split_qd, [SMEM] * 2 + [VMEM] * 3 + [ANY], [shaped(QD_ROWS, HD)] * 4, limit=WHOLE)(
        lengths[0, 0], owners[0, 0], queries[0], outputs[0], out_grads[0], kv[1]
    )
    qd_all = [qd[0]] + [shift(qd[k], "zl", k) for k in (1, 2, 3)]

    dq, codes, *dkv = call(
        attention_grads,
        8,
        [shaped(SLOTS, QROWS, HD), shaped(SLOTS, 16, HD)] + [shaped(4 * KV_ROWS, HD)] * 4,
        [
            pltpu.VMEM((SLOTS, QD_ROWS, HD), bf16),
            pltpu.VMEM((4, BLK, HD), bf16),
            pltpu.VMEM((4, BLK, HD), bf16),
            pltpu.VMEM((4, BLK, HD), f32),
            pltpu.VMEM((4, BLK, HD), f32),
            pltpu.VMEM((TOK, QROWS), jnp.int32),
        ],
        limit=LARGE,
    )(*kv_all, *qd_all)
    dkv_parts = [dkv[0]] + [shift(dkv[k], "y", 4 - k) for k in (1, 2, 3)]

    def to_owners(kernel, operands, heads):
        shape = (DOCS, SLOTS, CAP, heads * HD)
        rows = call(kernel, len(operands), shaped(*shape), out_specs=VMEM)(*operands)
        rows = rows.reshape(DOCS * SLOTS, CAP, heads * HD)
        rows = lax.all_to_all(rows, ("zh", "x", "c", "zl"), 0, 0, tiled=True)
        return rows.reshape(shape)

    query_rows = to_owners(pack_query, [dq, codes], GROUP)
    query_rows, *dkv_parts = lax.optimization_barrier((query_rows, *dkv_parts))
    kv_rows = to_owners(pack_kv, [codes, *dkv_parts], 2)
    returned = call(
        place,
        2,
        shaped(DOCS, CAP, (QH + 2 * KVH) * HD),
        [pltpu.SemaphoreType.DMA((3 * SLOTS,))],
        ANY,
    )(query_rows, kv_rows)
    return returned[None, None]


def solution(mesh):
    split = Mesh(mesh.devices.reshape(2, 4, 2, 4, 4), ("zh", "x", "c", "zl", "y"))
    rows = P(("zh", "x", "c"), ("zl", "y"), None)
    return jax.shard_map(
        body,
        mesh=split,
        in_specs=(rows,) * 7,
        out_specs=P(("zh", "x", "c"), ("zl", "y"), None, None, None),
        check_vma=False,
    )
```

```python
import functools

import jax
import jax.numpy as jnp
from jax import lax
from jax.experimental import pallas as pl
from jax.experimental.pallas import tpu as pltpu
from jax.sharding import Mesh, PartitionSpec as P

HD = 128
QH = 16
KVH = 4
GROUP = QH // KVH
TOK = 128
CAP = 16
DOCS = 16
CODE_ROW = 12
SLOTS = 4
BLK = SLOTS * TOK
QROWS = GROUP * TOK
QD_ROWS = 2 * QROWS + 16
KV_ROWS = 2 * TOK
FACTOR = HD ** (-0.5)
LOG2E = 1.4426950408889634
f32 = jnp.float32
bf16 = jnp.bfloat16
VMEM = pl.BlockSpec(memory_space=pltpu.VMEM)
SMEM = pl.BlockSpec(memory_space=pltpu.SMEM)
SMALL, LARGE, WHOLE = 12 * 2**20, 20 * 2**20, 56 * 2**20


def aligned(index, unit):
    return pl.ds(pl.multiple_of(index * unit, unit), unit)


def split_kv(k_ref, v_ref, *outs):
    z = lax.axis_index("zl")
    for slot in range(SLOTS):
        head = aligned(lax.rem(z + slot, SLOTS), HD)
        outs[slot][:TOK, :] = k_ref[:, head]
        outs[slot][TOK:, :] = v_ref[:, head]


def split_qd(lens_ref, owners_ref, q_ref, o_ref, g_ref, after_ref, *outs):
    z = lax.axis_index("zl")
    lane = lax.broadcasted_iota(jnp.int32, (TOK, HD), 1)
    position = lax.broadcasted_iota(jnp.int32, (16, TOK), 1)
    code = jnp.zeros((16, TOK), jnp.int32)
    start = 0
    for child in range(16):
        code = jnp.where(position >= start, owners_ref[child] * CAP + position - start, code)
        start = start + lens_ref[child]
    row = lax.broadcasted_iota(jnp.int32, (16, TOK), 0)
    code = jnp.where(row == CODE_ROW, code, 0).astype(f32)
    for slot in range(SLOTS):
        dest = lax.rem(z + slot, SLOTS)
        terms = jnp.zeros((TOK, HD), f32)
        for h in range(GROUP):
            head = aligned(dest * GROUP + h, HD)
            grad = g_ref[:, head]
            outs[slot][h * TOK : (h + 1) * TOK, :] = q_ref[:, head]
            outs[slot][QROWS + h * TOK : QROWS + (h + 1) * TOK, :] = grad
            term = jnp.sum(
                grad.astype(f32) * o_ref[:, head].astype(f32), axis=1, keepdims=True
            )
            terms = jnp.where(lax.rem(lane, GROUP) == h, term, terms)
        high = terms.astype(bf16).astype(f32)
        mid = (terms - high).astype(bf16).astype(f32)
        low = terms - high - mid
        part = lane // GROUP
        packed = jnp.where(
            part == 0, high, jnp.where(part == 1, mid, jnp.where(part == 2, low, 0.0))
        )
        outs[slot][2 * QROWS :, :] = (packed.T[:16, :] + code).astype(bf16)


def dot(a, b, dims):
    return lax.dot_general(a, b, (dims, ((), ())), preferred_element_type=f32)


def move(in_ref, out_ref):
    out_ref[...] = in_ref[...]


def attention_grads(*refs):
    kv_refs, qd_refs = refs[:4], refs[4:8]
    dq_ref, code_ref, dkv_refs = refs[8], refs[9], refs[10:14]
    qd, kk, vv, kacc, vacc, delta = refs[14:]
    y, z = lax.axis_index("y"), lax.axis_index("zl")
    along_z = [lax.rem(z + SLOTS - s, SLOTS) for s in range(SLOTS)]
    along_y = [aligned(lax.rem(y + SLOTS - k, SLOTS), TOK) for k in range(4)]
    for s in range(SLOTS):
        qd[along_z[s]] = qd_refs[s][...]
        for k in range(4):
            kk[along_z[s], along_y[k], :] = kv_refs[k][s * KV_ROWS : s * KV_ROWS + TOK, :]
            vv[along_z[s], along_y[k], :] = kv_refs[k][s * KV_ROWS + TOK : (s + 1) * KV_ROWS, :]
    key_at = lax.broadcasted_iota(jnp.int32, (TOK, QROWS), 0)
    query_at = lax.rem(lax.broadcasted_iota(jnp.int32, (TOK, QROWS), 1), TOK)
    delta[...] = key_at - query_at

    for part in range(SLOTS):
        query = qd[part, :QROWS, :]
        grad = qd[part, QROWS : 2 * QROWS, :]
        terms3 = qd[part, 2 * QROWS :, :].astype(f32)
        term4 = terms3[0:4] + terms3[4:8] + terms3[8:12]
        term = jnp.concatenate([term4[h : h + 1] for h in range(GROUP)], axis=1)
        scores = [dot(kk[t], query, ((1,), (1,))) for t in range(part + 1)]
        scores[part] = jnp.concatenate(
            [
                jnp.where(
                    delta[...] <= (y - other) * TOK,
                    scores[part][other * TOK : (other + 1) * TOK],
                    -jnp.inf,
                )
                for other in range(SLOTS)
            ],
            axis=0,
        )
        top = functools.reduce(
            jnp.maximum, [jnp.max(score, axis=0, keepdims=True) for score in scores]
        )
        weights = [jnp.exp2((score - top) * (FACTOR * LOG2E)) for score in scores]
        inverse = 1.0 / sum(jnp.sum(weight, axis=0, keepdims=True) for weight in weights)
        dq = jnp.zeros((QROWS, HD), f32)
        for t in range(part + 1):
            attn = weights[t] * inverse
            grad_attn = dot(vv[t], grad, ((1,), (1,)))
            low = (attn * (grad_attn - term)).astype(bf16)
            value_part = dot(attn.astype(bf16), grad, ((1,), (0,)))
            key_part = dot(low, query, ((1,), (0,)))
            if t == part:
                vacc[t] = value_part
                kacc[t] = key_part
            else:
                vacc[t] += value_part
                kacc[t] += key_part
            dq = dq + dot(low, kk[t], ((0,), (0,)))
        dq_ref[part] = (dq * FACTOR).astype(bf16)
        code_ref[part] = qd[part, 2 * QROWS :, :]

    for t in range(SLOTS):
        for k in range(4):
            keys = kacc[t, along_y[k], :]
            dkv_refs[k][t * KV_ROWS : t * KV_ROWS + TOK, :] = (keys * FACTOR).astype(bf16)
            values = vacc[t, along_y[k], :]
            dkv_refs[k][t * KV_ROWS + TOK : (t + 1) * KV_ROWS, :] = values.astype(bf16)


def pick(code_ref, t, heads, out_ref):
    slot_code = lax.broadcasted_iota(jnp.int32, (DOCS * CAP, TOK), 0)
    code = code_ref[t].astype(f32)[CODE_ROW : CODE_ROW + 1].astype(jnp.int32)
    sel = jnp.where(slot_code == code, 1.0, 0.0).astype(bf16)
    for place, rows in enumerate(heads):
        picked = dot(sel, rows, ((1,), (0,))).astype(bf16)
        out_ref[:, t, :, place * HD : (place + 1) * HD] = picked.reshape(DOCS, CAP, HD)


def pack_query(dq_ref, code_ref, out_ref):
    for t in range(SLOTS):
        pick(code_ref, t, [dq_ref[t, h * TOK : (h + 1) * TOK, :] for h in range(GROUP)], out_ref)


def pack_kv(code_ref, own_ref, one_ref, two_ref, three_ref, out_ref):
    total = own_ref[...].astype(f32) + one_ref[...].astype(f32)
    total = (total + two_ref[...].astype(f32) + three_ref[...].astype(f32)).astype(bf16)
    for t in range(SLOTS):
        first = t * KV_ROWS
        heads = [total[first : first + TOK], total[first + TOK : first + KV_ROWS]]
        pick(code_ref, t, heads, out_ref)


def place(query_ref, kv_ref, out, sem):
    copies = []
    for group in range(SLOTS):
        for source, first, width, to in (
            (query_ref, 0, QROWS, group * GROUP * HD),
            (kv_ref, 0, HD, (QH + group) * HD),
            (kv_ref, HD, HD, (QH + KVH + group) * HD),
        ):
            copies.append(
                pltpu.make_async_copy(
                    source.at[:, group, :, pl.ds(first, width)],
                    out.at[:, :, pl.ds(to, width)],
                    sem.at[len(copies)],
                )
            )
    for copy in copies:
        copy.start()
    for copy in copies:
        copy.wait()


ANY = pl.BlockSpec(memory_space=pl.ANY)


def call(kernel, ins, outs, scratch=(), out_specs=None, aliases=None, limit=SMALL):
    return pl.pallas_call(
        kernel,
        out_shape=outs,
        in_specs=[VMEM] * ins if isinstance(ins, int) else ins,
        out_specs=out_specs or [VMEM] * len(outs),
        scratch_shapes=list(scratch),
        input_output_aliases=aliases or {},
        compiler_params=pltpu.CompilerParams(vmem_limit_bytes=limit),
    )


def shaped(*shape, dtype=bf16):
    return jax.ShapeDtypeStruct(shape, dtype)


def body(queries, keys, values, outputs, out_grads, lengths, owners):
    def shift(a, axis, by):
        size = lax.axis_size(axis)
        return lax.ppermute(a, axis, [(i, (i + by) % size) for i in range(size)])

    kv = call(split_kv, 2, [shaped(KV_ROWS, HD)] * 4, limit=WHOLE)(keys[0], values[0])
    kv_own = jnp.concatenate([kv[0]] + [shift(kv[k], "zl", k) for k in (1, 2, 3)], axis=0)
    qd = call(split_qd, [SMEM] * 2 + [VMEM] * 3 + [ANY], [shaped(QD_ROWS, HD)] * 4, limit=WHOLE)(
        lengths[0, 0], owners[0, 0], queries[0], outputs[0], out_grads[0], kv[1]
    )
    own = call(move, 1, shaped(QD_ROWS, HD), out_specs=VMEM)(qd[0])
    own, kv_late = lax.optimization_barrier((own, kv_own))
    kv_all = [kv_own] + [shift(kv_late if k == 1 else kv_own, "y", k) for k in (1, 2, 3)]
    qd_all = [own] + [shift(qd[k], "zl", k) for k in (1, 2, 3)]

    dq, codes, *dkv = call(
        attention_grads,
        8,
        [shaped(SLOTS, QROWS, HD), shaped(SLOTS, 16, HD)] + [shaped(4 * KV_ROWS, HD)] * 4,
        [
            pltpu.VMEM((SLOTS, QD_ROWS, HD), bf16),
            pltpu.VMEM((4, BLK, HD), bf16),
            pltpu.VMEM((4, BLK, HD), bf16),
            pltpu.VMEM((4, BLK, HD), f32),
            pltpu.VMEM((4, BLK, HD), f32),
            pltpu.VMEM((TOK, QROWS), jnp.int32),
        ],
        limit=LARGE,
    )(*kv_all, *qd_all)
    dkv_parts = [dkv[0]] + [shift(dkv[k], "y", 4 - k) for k in (1, 2, 3)]

    def to_owners(kernel, operands, heads):
        shape = (DOCS, SLOTS, CAP, heads * HD)
        rows = call(kernel, len(operands), shaped(*shape), out_specs=VMEM)(*operands)
        rows = rows.reshape(DOCS * SLOTS, CAP, heads * HD)
        rows = lax.all_to_all(rows, ("zh", "x", "c", "zl"), 0, 0, tiled=True)
        return rows.reshape(shape)

    query_rows = to_owners(pack_query, [dq, codes], GROUP)
    query_rows, *dkv_parts = lax.optimization_barrier((query_rows, *dkv_parts))
    kv_rows = to_owners(pack_kv, [codes, *dkv_parts], 2)
    returned = call(
        place,
        2,
        shaped(DOCS, CAP, (QH + 2 * KVH) * HD),
        [pltpu.SemaphoreType.DMA((3 * SLOTS,))],
        ANY,
    )(query_rows, kv_rows)
    return returned[None, None]


def solution(mesh):
    split = Mesh(mesh.devices.reshape(2, 4, 2, 4, 4), ("zh", "x", "c", "zl", "y"))
    rows = P(("zh", "x", "c"), ("zl", "y"), None)
    return jax.shard_map(
        body,
        mesh=split,
        in_specs=(rows,) * 7,
        out_specs=P(("zh", "x", "c"), ("zl", "y"), None, None, None),
        check_vma=False,
    )
```
